32 devices in a mesh: groups: 2 (over y), mp: 16 (over z, x, core).
Axes of the slice: x: 2, y: 2, z: 4, core: 2. Of those that a mesh axis runs over, the one named last changes fastest.
Arguments:
- hidden_in: bfloat16 [128, 18432], P('groups', 'mp'), parts along dimension 0, may hold values from -128 to 128
- w_qkv: bfloat16 [16, 9216, 1600], P('mp'), may hold values from -0.046875 to 0.046875
- w_out: bfloat16 [16, 1536, 9216], P('mp'), may hold values from -0.3125 to 0.3125
- key_cache: bfloat16 [128, 1792, 256], P(('groups', 'mp')), parts along dimension 0, may hold values from -256 to 256
- value_cache: bfloat16 [128, 1792, 256], P(('groups', 'mp')), parts along dimension 0, may hold values from -6 to 6
- lengths: int32 [128], P(('groups', 'mp')), parts along dimension 0, may hold values from 1 to 1792, as said below
Outputs:
- outputs: bfloat16 [128, 18432], P('groups', 'mp'), parts along dimension 0
The draws below stay inside these ranges and needn't reach their ends.
There are 2 independent parts, one for each index of `groups`. The reference program is written for one: setup_inputs(seed, part) draws one part's arguments, and reference() takes and returns one part's arrays. A program takes and returns all parts, laid end to end along the dimension named above; an argument that names none is the same for every part. Nothing has to cross between parts.
Inputs may be any that keep to these rules, and one draw needn't show every extreme that they name: `lengths`: every row has at least one cached token; in each part some row holds exactly 1792.
All inputs are finite; a program needn't handle non-finite values.
Results may differ from the reference program's by a relative error of at most 0.012.
The reference program's roundings to bfloat16 on the way (of `weights` and `attended`) count: a program that leaves them out, or rounds other values in their place, can miss the bound.
Values may be sent and summed in bfloat16 or wider, within the bound.
A program may use at most 192 MiB of HBM per device.

```python
import jax
import jax.numpy as jnp
from jax import lax

D = 18432
HEAD_DIM = 256
CTX = 1792
QW = 12288
COLS = 12800
COL_GRP = 8
ROW_GRP = 2
ROWS = 64
N_MP = 16


def draw_hidden_in(key, part):
    key = jax.random.fold_in(key, 11)
    keys_all = jax.random.split(key, 4)
    row_scale = jnp.exp(jax.random.uniform(keys_all[0], (ROWS, 1), minval=jnp.log(0.5), maxval=jnp.log(5.0)))
    column_rise = 3.0 ** (jnp.arange(D, dtype=jnp.float32) / (D - 1))
    column_scale = column_rise[None, :] * jnp.exp(jax.random.uniform(keys_all[1], (1, D), minval=jnp.log(0.6), maxval=jnp.log(2.0)))
    jitter = jnp.clip(jax.random.normal(keys_all[2], (ROWS, D)), -4.0, 4.0)
    offset = jax.random.uniform(keys_all[3], (ROWS, 1), minval=-1.5, maxval=1.5)
    return ((offset + jitter * column_scale) * row_scale).astype(jnp.bfloat16)


def draw_key_cache(key, part):
    key = jax.random.fold_in(key, 23)
    keys_all = jax.random.split(key, 2)
    shape_half = (ROWS, CTX // 2, 1, HEAD_DIM)
    base_keys = jnp.clip(jax.random.normal(keys_all[0], shape_half), -6.0, 6.0)
    second_keys = jnp.clip(jax.random.normal(keys_all[1], shape_half), -6.0, 6.0)
    paired = jnp.concatenate([base_keys, second_keys], 2)
    return paired.reshape(ROWS, CTX, HEAD_DIM).astype(jnp.bfloat16)


def draw_lengths(key, part):
    key = jax.random.fold_in(key, 37)
    keys_all = jax.random.split(key, 3)
    first_draw = jax.random.randint(keys_all[0], (ROWS,), 0, CTX)
    second_draw = jax.random.randint(keys_all[1], (ROWS,), 0, CTX)
    counts = 1 + first_draw * second_draw // CTX
    chosen = jax.random.randint(keys_all[2], (), 0, ROWS)
    return jnp.where(jnp.arange(ROWS) == chosen, CTX, counts).astype(jnp.int32)


def levels(rng, extent, cuts, least, high):
    def one(position, shards_of):
        steps = jax.random.uniform(jax.random.fold_in(jax.random.fold_in(rng, 6), position), (shards_of,), jnp.float32, least / len(cuts), high / len(cuts))
        return jnp.repeat(jnp.exp(steps), extent[position] // shards_of).reshape((-1,) + (1,) * (len(extent) - position - 1))

    loudness = one(*cuts[0])
    for cut in cuts[1:]:
        loudness = loudness * one(*cut)
    return loudness


def scatter_about(rng, extent, width, bound, cuts=(), held_as=jnp.bfloat16):
    entries = jax.random.normal(rng, extent, jnp.float32) * width
    if len(cuts) > 0:
        entries = levels(rng, extent, cuts, -0.22, 0.18) * entries
    return jnp.clip(entries, min=-bound, max=bound).astype(held_as)


def setup_inputs(seed: int = 0, part: int = 0) -> dict:
    seeds = jax.random.split(jax.random.key(seed), 7)
    part_keys = jax.random.split(jax.random.fold_in(seeds[6], part), 7)
    return {
        "hidden_in": draw_hidden_in(jax.random.fold_in(jax.random.fold_in(seeds[6], part), 71), part),
        "w_qkv": scatter_about(seeds[1], (N_MP, D // ROW_GRP, COLS // COL_GRP), D ** -0.5, 0.046875, ((0, 16),)),
        "w_out": scatter_about(seeds[2], (N_MP, QW // COL_GRP, D // ROW_GRP), (QW // 32) ** -0.5, 0.3125, ((0, 16),)),
        "key_cache": draw_key_cache(jax.random.fold_in(jax.random.fold_in(seeds[6], part), 71), part),
        "value_cache": scatter_about(part_keys[4], (ROWS, CTX, HEAD_DIM), 1.0, 6.0, ((0, 16),)),
        "lengths": draw_lengths(jax.random.fold_in(jax.random.fold_in(seeds[6], part), 71), part),
    }


def rotate(vectors, angle_now):
    half_dim = vectors.shape[-1] // 2
    front_half = vectors[..., :half_dim]
    back_half = vectors[..., half_dim:]
    cosine = jnp.cos(angle_now)
    sine_part = jnp.sin(angle_now)
    return jnp.concatenate([front_half * cosine - back_half * sine_part, back_half * cosine + front_half * sine_part], -1)

def attend(projected, key_block, value_block, row_lengths):
    row_count = projected.shape[0]
    head_size = key_block.shape[-1]
    head_count = (projected.shape[1] - 2 * head_size) // head_size
    half_dim = head_size // 2
    frequency = 10000.0 ** (-jnp.arange(half_dim, dtype=jnp.float32) / half_dim)
    angle_now = row_lengths.astype(jnp.float32)[:, None] * frequency[None, :]
    width_q = head_count * head_size
    queries = rotate(projected[:, :width_q].reshape(row_count, head_count, head_size), angle_now[:, None, :]).astype(jnp.bfloat16)
    new_key = rotate(projected[:, width_q:width_q + head_size], angle_now).astype(jnp.bfloat16)
    new_value = projected[:, width_q + head_size:].astype(jnp.bfloat16)
    score_scale = 1.0 / jnp.sqrt(jnp.float32(head_size))
    scores = jnp.einsum('bhd,btd->bht', queries.astype(jnp.float32), key_block.astype(jnp.float32)) * score_scale
    live_mask = jnp.arange(key_block.shape[1])[None, None, :] < row_lengths[:, None, None]
    scores = jnp.where(live_mask, scores, -1e+30)
    own_score = lax.optimization_barrier(jnp.sum(queries.astype(jnp.float32) * new_key.astype(jnp.float32)[:, None, :], -1)) * score_scale
    largest = jnp.maximum(lax.optimization_barrier(jnp.max(scores, -1)), own_score)
    weights = jnp.exp(scores - largest[..., None])
    own_weight = jnp.exp(own_score - largest)
    denominator = lax.optimization_barrier(jnp.sum(weights, -1)) + own_weight
    blended = jnp.einsum('bht,btd->bhd', weights.astype(jnp.bfloat16).astype(jnp.float32), value_block.astype(jnp.float32))
    blended = blended + own_weight.astype(jnp.bfloat16).astype(jnp.float32)[..., None] * new_value.astype(jnp.float32)[:, None, :]
    return (blended / denominator[..., None]).reshape(row_count, width_q).astype(jnp.bfloat16)

def reference(hidden_in, w_qkv, w_out, key_cache, value_cache, lengths):
    qkv_full = w_qkv.reshape(ROW_GRP, COL_GRP, D // ROW_GRP, COLS // COL_GRP).transpose(0, 2, 1, 3).reshape(D, COLS)
    out_full = w_out.reshape(ROW_GRP, COL_GRP, QW // COL_GRP, D // ROW_GRP).transpose(1, 2, 0, 3).reshape(QW, D)
    wide_in = hidden_in.astype(jnp.float32)
    row_mean = lax.optimization_barrier(jnp.sum(wide_in, 1)) / D
    variance = lax.optimization_barrier(jnp.sum(wide_in * wide_in, 1)) / D - row_mean * row_mean
    inverse = lax.rsqrt(variance + 1e-05)
    column_total = lax.optimization_barrier(jnp.sum(qkv_full.astype(jnp.float32), 0))
    raw_sums = jnp.dot(hidden_in, qkv_full, preferred_element_type=jnp.float32)
    projected = inverse[:, None] * (raw_sums - row_mean[:, None] * column_total[None, :])

    def one_row(row_items):
        proj_row, key_row, value_row, length_row = row_items
        return attend(proj_row[None], key_row[None], value_row[None], length_row[None])[0]
    attended = lax.map(one_row, (projected, key_cache, value_cache, lengths))
    return jnp.dot(attended, out_full, preferred_element_type=jnp.float32).astype(jnp.bfloat16)
```

```python
import jax
import jax.numpy as jnp
from jax import lax
from jax.experimental import pallas as pl
from jax.experimental.pallas import tpu as pltpu
from jax.sharding import PartitionSpec as P

MESH = pl.DeviceIdType.MESH
D = 18432
COL_BITS = 3


def swapped(value, axis, bit):
    mask = 2**bit
    pairs = [(source, source ^ mask) for source in range(lax.axis_size(axis))]
    return lax.ppermute(value, axis, pairs)


def rotate(vectors, angle_now):
    half_dim = vectors.shape[-1] // 2
    front_half = vectors[..., :half_dim]
    back_half = vectors[..., half_dim:]
    cosine = jnp.cos(angle_now)
    sine_part = jnp.sin(angle_now)
    return jnp.concatenate(
        [front_half * cosine - back_half * sine_part, back_half * cosine + front_half * sine_part],
        -1,
    )


def cache_scores(query_part, key_cache, lengths):
    row_count = query_part.shape[0]
    head_size = key_cache.shape[-1]
    head_count = query_part.shape[1] // head_size
    half_dim = head_size // 2
    frequency = 10000.0 ** (-jnp.arange(half_dim, dtype=jnp.float32) / half_dim)
    angle_now = lengths.astype(jnp.float32)[:, None] * frequency[None, :]
    queries = rotate(
        query_part.reshape(row_count, head_count, head_size), angle_now[:, None, :]
    ).astype(jnp.bfloat16)
    score_scale = 1.0 / jnp.sqrt(jnp.float32(head_size))
    scores = (
        jnp.einsum("bhd,btd->bht", queries, key_cache, preferred_element_type=jnp.float32)
        * score_scale
    )
    live_mask = jnp.arange(key_cache.shape[1])[None, None, :] < lengths[:, None, None]
    return (queries, angle_now, jnp.where(live_mask, scores, -1e30))


def finish(queries, angle_now, scores, keyval_part, value_cache):
    row_count, head_count, head_size = queries.shape
    new_key = rotate(keyval_part[:, :head_size], angle_now).astype(jnp.bfloat16)
    new_value = keyval_part[:, head_size:].astype(jnp.bfloat16)
    score_scale = 1.0 / jnp.sqrt(jnp.float32(head_size))
    own_score = (
        jnp.sum(queries.astype(jnp.float32) * new_key.astype(jnp.float32)[:, None, :], -1)
        * score_scale
    )
    largest = jnp.maximum(jnp.max(scores, -1), own_score)
    weights = jnp.exp(scores - largest[..., None])
    own_weight = jnp.exp(own_score - largest)
    denominator = jnp.sum(weights, -1) + own_weight
    blended = jnp.einsum(
        "bht,btd->bhd",
        weights.astype(jnp.bfloat16),
        value_cache,
        preferred_element_type=jnp.float32,
    )
    blended = (
        blended
        + own_weight.astype(jnp.bfloat16).astype(jnp.float32)[..., None]
        * new_value.astype(jnp.float32)[:, None, :]
    )
    return (
        (blended / denominator[..., None])
        .reshape(row_count, head_count * head_size)
        .astype(jnp.bfloat16)
    )


def gather_features(block):
    device_index = lax.axis_index("mp")
    gathered = block
    for bit_level in range(COL_BITS):
        incoming = swapped(gathered, "mp", bit_level)
        mine_bit = device_index >> bit_level & 1
        gathered = jnp.where(
            mine_bit == 1,
            jnp.concatenate([incoming, gathered], 1),
            jnp.concatenate([gathered, incoming], 1),
        )
    return gathered


def reduce_rows(partial_value, high_bits):
    device_index = lax.axis_index("mp")
    total = partial_value
    for bit_level in reversed(range(COL_BITS, COL_BITS + high_bits)):
        half_rows = total.shape[0] // 2
        keep_back = device_index >> bit_level & 1 == 1
        outgoing = jnp.where(keep_back, total[:half_rows], total[half_rows:])
        staying = jnp.where(keep_back, total[half_rows:], total[:half_rows])
        total = staying + swapped(outgoing, "mp", bit_level)
    return total


def slots_to_holders(slots):
    device_index = lax.axis_index("mp")
    slot_count, row_count, width = slots.shape
    for bit_level in range(COL_BITS):
        shaped = slots.reshape(slot_count >> bit_level + 1, 2, 1 << bit_level, row_count, width)
        mine_bit = device_index >> bit_level & 1
        front_slots = shaped[:, 0]
        back_slots = shaped[:, 1]
        outgoing = jnp.where(mine_bit == 1, front_slots, back_slots)
        incoming = swapped(outgoing, "mp", bit_level)
        new_front = jnp.where(mine_bit == 1, incoming, front_slots)
        new_back = jnp.where(mine_bit == 1, back_slots, incoming)
        slots = jnp.stack([new_front, new_back], 1).reshape(slot_count, row_count, width)
    return slots


def reduce_features(partial_value):
    device_index = lax.axis_index("mp")
    total = partial_value
    for bit_level in reversed(range(COL_BITS)):
        half_cols = total.shape[1] // 2
        keep_back = device_index >> bit_level & 1 == 1
        outgoing = jnp.where(keep_back, total[:, :half_cols], total[:, half_cols:])
        staying = jnp.where(keep_back, total[:, half_cols:], total[:, :half_cols])
        total = staying + swapped(outgoing, "mp", bit_level)
    return total


def shards_plain(hidden_in, w_qkv, w_out, key_cache, value_cache, lengths):
    qkv_tile = w_qkv[0]
    out_tile = w_out[0]
    own_rows = key_cache.shape[0]
    head_size = key_cache.shape[2]
    tile_count = 1 << COL_BITS
    col_width = qkv_tile.shape[1]
    full_cols = col_width * tile_count
    width_q = full_cols - 2 * head_size
    head_width = out_tile.shape[0]
    high_bits = lax.axis_size("mp").bit_length() - 1 - COL_BITS
    device_index = lax.axis_index("mp")
    column_block = device_index & tile_count - 1
    wide_in = hidden_in.astype(jnp.float32)
    sums_local = jnp.sum(wide_in, 1)
    squares_local = jnp.sum(wide_in * wide_in, 1)
    ones_row = jnp.ones((1, qkv_tile.shape[0]), jnp.bfloat16)
    tile_columns = jnp.dot(ones_row, qkv_tile, preferred_element_type=jnp.float32)[0]
    columns_local = lax.dynamic_update_slice_in_dim(
        jnp.zeros((full_cols,), jnp.float32), tile_columns, column_block * col_width, 0
    )
    sums_all, squares_all, column_total = lax.psum((sums_local, squares_local, columns_local), "mp")
    first_row = device_index * own_rows
    row_sums = lax.dynamic_slice_in_dim(sums_all, first_row, own_rows)
    row_squares = lax.dynamic_slice_in_dim(squares_all, first_row, own_rows)
    row_mean = row_sums / D
    variance = row_squares / D - row_mean * row_mean
    inverse = lax.rsqrt(variance + 1e-05)
    feature_block = gather_features(hidden_in)
    partial_value = jnp.dot(feature_block, qkv_tile, preferred_element_type=jnp.float32)
    group_rows = reduce_rows(partial_value, high_bits)
    slots = group_rows.reshape(tile_count, own_rows, col_width)
    arrived = slots_to_holders(slots)
    raw_sums = jnp.transpose(arrived, (1, 0, 2)).reshape(own_rows, full_cols)
    projected = inverse[:, None] * (raw_sums - row_mean[:, None] * column_total[None, :])
    queries, angle_now, scores = cache_scores(projected[:, :width_q], key_cache, lengths)
    attended = finish(queries, angle_now, scores, projected[:, width_q:], value_cache)
    block_cols = lax.dynamic_slice_in_dim(
        lax.all_gather(attended, "mp", axis=0, tiled=True), column_block * head_width, head_width, 1
    )
    partial_out = jnp.dot(block_cols, out_tile, preferred_element_type=jnp.float32)
    outputs = reduce_features(partial_out)
    return outputs.astype(jnp.bfloat16)


RING = 4


def flipped(index, flips, bits):
    total = 0
    for level in range(bits):
        own_bit = index // 2**level % 2
        flip_bit = flips // 2**level % 2
        total = total + (own_bit + flip_bit - 2 * own_bit * flip_bit) * 2**level
    return total


def block_kernel(
    hid_ref, cos_ref, sin_ref, len_ref, wq_hbm, wo_hbm, key_hbm, val_hbm, out_ref,
    xb, wb, acc, stat_send, stat_recv, psb, prb, pj, qf, attf, msgf, dsb, drb, lhsf, lhs,
    keys, vals, wo, pbuf, erecv, irecv,
    w_sem, kv_sem, wo_sem, xs_sem, xr_sem, ss_sem, sr_sem, ps_sem, pr_sem,
    ds_sem, dr_sem, es_sem, er_sem, is_sem, ir_sem,
):
    me = lax.axis_index("mp")
    low = me % 8
    high = me // 8 * 8
    part_rows, feats = hid_ref.shape
    own_rows = cos_ref.shape[0]
    col_width = acc.shape[1]
    head_size = qf.shape[2]
    head_count = qf.shape[1]
    half_dim = head_size // 2
    width_q = head_count * head_size
    out_cols = wo.shape[2]
    n_dev = 16

    def w_copy(step, slot):
        rows = pl.ds(pl.multiple_of(flipped(low, step, 3) * feats, feats), feats)
        return pltpu.make_async_copy(wq_hbm.at[0, rows], wb.at[slot], w_sem.at[slot])

    def wo_copy(block):
        cols = pl.ds(block * out_cols, out_cols)
        return pltpu.make_async_copy(wo_hbm.at[0, :, cols], wo.at[block], wo_sem.at[block])

    key_copy = pltpu.make_async_copy(key_hbm, keys, kv_sem.at[0])
    val_copy = pltpu.make_async_copy(val_hbm, vals, kv_sem.at[1])

    for step in range(RING):
        w_copy(step, step).start()

    barrier = pltpu.get_barrier_semaphore()
    for flips in range(1, n_dev):
        pl.semaphore_signal(
            barrier, inc=1, device_id={"mp": flipped(me, flips, 4)}, device_id_type=MESH
        )
    pl.semaphore_wait(barrier, n_dev - 1)

    def x_copy(source, flips, slot):
        return pltpu.make_async_remote_copy(
            src_ref=source, dst_ref=xb.at[slot], send_sem=xs_sem.at[slot],
            recv_sem=xr_sem.at[slot], device_id={"mp": high + flipped(low, flips, 3)},
            device_id_type=MESH,
        )

    for flips in (2, 4, 6, 1):
        x_copy(hid_ref, flips, flips).start()
    xb[0] = hid_ref[...]
    acc[...] = jnp.zeros_like(acc)

    stat_copy = pltpu.make_async_remote_copy(
        src_ref=stat_send, dst_ref=stat_recv, send_sem=ss_sem, recv_sem=sr_sem,
        device_id={"mp": flipped(me, 8, 4)}, device_id_type=MESH,
    )

    def step_body(step, sums):
        total, squares = sums
        slot = step % RING

        @pl.when(step > 0)
        def _():
            x_copy(xb.at[step], 1, step).wait_recv()

        @pl.when((step >= 2) & (step % 2 == 0))
        def _():
            x_copy(xb.at[step], 1, step + 1).start()

        features = xb[step]
        wide = features.astype(jnp.float32)
        total = total + jnp.sum(wide, 1, keepdims=True)
        squares = squares + jnp.sum(wide * wide, 1, keepdims=True)

        @pl.when(step == 7)
        def _():
            lane = lax.broadcasted_iota(jnp.int32, stat_send.shape, 1)
            stat_send[...] = jnp.where(lane < 64, total, squares)
            stat_copy.start()

        w_copy(step, slot).wait()
        with_ones = jnp.concatenate([features, jnp.ones((16, feats), jnp.bfloat16)], 0)
        acc[...] += jnp.dot(with_ones, wb[slot], preferred_element_type=jnp.float32)

        @pl.when(step + RING < 8)
        def _():
            w_copy(step + RING, slot).start()

        @pl.when(step == 3)
        def _():
            key_copy.start()
            val_copy.start()
            for block in range(4):
                wo_copy(block).start()

        @pl.when(step == 5)
        def _():
            for block in range(4, 8):
                wo_copy(block).start()

        return (total, squares)

    nothing = jnp.zeros((part_rows, 1), jnp.float32)
    lax.fori_loop(0, 8, step_body, (nothing, nothing))
    stat_copy.wait()
    both = stat_send[...] + stat_recv[...]
    row_mean = both[:, :1] / D
    variance = both[:, 64:65] / D - row_mean * row_mean
    inverse = lax.rsqrt(variance + 1e-05)
    projected = inverse * (acc[:part_rows] - row_mean * acc[part_rows : part_rows + 1])
    for dev in range(n_dev):
        psb[dev] = projected[dev * own_rows : (dev + 1) * own_rows]

    def p_copy(flips):
        target = flipped(me, flips, 4)
        return pltpu.make_async_remote_copy(
            src_ref=psb.at[target], dst_ref=prb.at[me], send_sem=ps_sem.at[flips],
            recv_sem=pr_sem.at[flips], device_id={"mp": target}, device_id_type=MESH,
        )

    def p_arrival(flips):
        source = flipped(me, flips, 4)
        return pltpu.make_async_remote_copy(
            src_ref=psb.at[source], dst_ref=prb.at[source], send_sem=ps_sem.at[flips],
            recv_sem=pr_sem.at[flips], device_id={"mp": source}, device_id_type=MESH,
        )

    for flips in range(n_dev - 1, 0, -1):
        p_copy(flips).start()
    prb[me] = psb[me]
    for flips in range(1, n_dev):
        p_arrival(flips).wait_recv()
    for block in range(8):
        pj[:, block * col_width : (block + 1) * col_width] = prb[block] + prb[block + 8]
    for head in range(head_count):
        for row in range(own_rows):
            qf[row, head : head + 1, :] = pj[
                row : row + 1, head * head_size : (head + 1) * head_size
            ]

    key_copy.wait()
    val_copy.wait()
    scale = 1.0 / 16.0 if head_size == 256 else head_size**-0.5

    def turned(vectors, cosine, sine):
        front, back = vectors[:, :half_dim], vectors[:, half_dim:]
        return jnp.concatenate([front * cosine - back * sine, back * cosine + front * sine], 1)

    for row in range(own_rows):
        cosine, sine = cos_ref[row : row + 1], sin_ref[row : row + 1]
        queries = turned(qf[row], cosine, sine).astype(jnp.bfloat16)
        new_key = turned(pj[row : row + 1, width_q : width_q + head_size], cosine, sine)
        new_key = new_key.astype(jnp.bfloat16).astype(jnp.float32)
        new_value = pj[row : row + 1, width_q + head_size :]
        new_value = new_value.astype(jnp.bfloat16).astype(jnp.float32)
        scores = scale * lax.dot_general(
            queries, keys[row], (((1,), (1,)), ((), ())), preferred_element_type=jnp.float32
        )
        slots = lax.broadcasted_iota(jnp.int32, scores.shape, 1)
        scores = jnp.where(slots < len_ref[row : row + 1, :1], scores, -1e30)
        own_score = scale * jnp.sum(queries.astype(jnp.float32) * new_key, 1, keepdims=True)
        largest = jnp.maximum(jnp.max(scores, 1, keepdims=True), own_score)
        weights = jnp.exp(scores - largest)
        own_weight = jnp.exp(own_score - largest)
        denominator = jnp.sum(weights, 1, keepdims=True) + own_weight
        blended = jnp.dot(
            weights.astype(jnp.bfloat16), vals[row], preferred_element_type=jnp.float32
        )
        blended = blended + own_weight.astype(jnp.bfloat16).astype(jnp.float32) * new_value
        attf[row] = blended / denominator

    parts = msgf.shape[1] // own_rows
    tiles = msgf.shape[2] // 128
    for block in range(8):
        for part in range(parts):
            for tile in range(tiles):
                column = ((block * parts + part) * tiles + tile) * 128
                head, lane = column // head_size, column % head_size
                for row in range(own_rows):
                    at = part * own_rows + row
                    msgf[block, at : at + 1, tile * 128 : (tile + 1) * 128] = attf[
                        row, head : head + 1, lane : lane + 128
                    ]
        dsb[block] = msgf[block].astype(jnp.bfloat16)

    def d_copy(flips):
        target = flipped(me, flips, 4)
        return pltpu.make_async_remote_copy(
            src_ref=dsb.at[target % 8], dst_ref=drb.at[me], send_sem=ds_sem.at[flips],
            recv_sem=dr_sem.at[flips], device_id={"mp": target}, device_id_type=MESH,
        )

    def d_arrival(flips):
        source = flipped(me, flips, 4)
        return pltpu.make_async_remote_copy(
            src_ref=dsb.at[source % 8], dst_ref=drb.at[source], send_sem=ds_sem.at[flips],
            recv_sem=dr_sem.at[flips], device_id={"mp": source}, device_id_type=MESH,
        )

    for flips in range(n_dev - 1, 0, -1):
        d_copy(flips).start()
    drb[me] = dsb[low]
    for flips in range(1, n_dev):
        d_arrival(flips).wait_recv()
    width = msgf.shape[2]
    for dev in range(n_dev):
        arrived = drb[dev].astype(jnp.float32)
        for part in range(parts):
            lhsf[dev * own_rows : (dev + 1) * own_rows, part * width : (part + 1) * width] = (
                arrived[part * own_rows : (part + 1) * own_rows]
            )
    lhs[...] = lhsf[...].astype(jnp.bfloat16)
    for block in range(8):
        wo_copy(block).wait()

    def e_copy(turn):
        return pltpu.make_async_remote_copy(
            src_ref=pbuf.at[2 * turn], dst_ref=erecv.at[turn], send_sem=es_sem.at[turn],
            recv_sem=er_sem.at[turn], device_id={"mp": flipped(me, 1, 4)}, device_id_type=MESH,
        )

    def i_copy(turn):
        return pltpu.make_async_remote_copy(
            src_ref=pbuf.at[2 * turn + 1], dst_ref=irecv.at[turn], send_sem=is_sem.at[turn],
            recv_sem=ir_sem.at[turn],
            device_id={"mp": high + flipped(low, 6 - 2 * turn, 3)}, device_id_type=MESH,
        )

    def out_body(turn, carry):
        flips = 6 - 2 * turn
        pbuf[2 * turn] = jnp.dot(
            lhs[...], wo[flipped(low, flips + 1, 3)], preferred_element_type=jnp.float32
        )
        e_copy(turn).start()
        pbuf[2 * turn + 1] = jnp.dot(
            lhs[...], wo[flipped(low, flips, 3)], preferred_element_type=jnp.float32
        )
        e_copy(turn).wait_recv()
        pbuf[2 * turn + 1] += erecv[turn]

        @pl.when(turn < 3)
        def _():
            i_copy(turn).start()

        return carry

    lax.fori_loop(0, 4, out_body, 0)
    for turn in range(3):
        i_copy(turn).wait_recv()
    out_ref[...] = (pbuf[7] + irecv[0] + irecv[1] + irecv[2]).astype(jnp.bfloat16)

    for slot in range(1, 8):
        x_copy(hid_ref, 1, slot).wait_send()
    for flips in range(1, n_dev):
        p_copy(flips).wait_send()
        d_copy(flips).wait_send()
    for turn in range(4):
        e_copy(turn).wait_send()
    for turn in range(3):
        i_copy(turn).wait_send()


def shards(hidden_in, w_qkv, w_out, key_cache, value_cache, lengths):
    part_rows, feats = hidden_in.shape
    own_rows, slot_count, head_size = key_cache.shape
    _, w_rows, col_width = w_qkv.shape
    _, head_width, out_width = w_out.shape
    if (
        lax.axis_size("mp") != 16
        or w_rows != 8 * feats
        or own_rows != 4
        or part_rows != 64
        or feats % 128 != 0
        or head_width % 512 != 0
        or head_size != 256
    ):
        return shards_plain(hidden_in, w_qkv, w_out, key_cache, value_cache, lengths)
    half_dim = head_size // 2
    out_cols = out_width // 8
    full_cols = col_width * 8
    head_count = head_width * 8 // head_size
    frequency = 10000.0 ** (-jnp.arange(half_dim, dtype=jnp.float32) / half_dim)
    angle_now = lengths.astype(jnp.float32)[:, None] * frequency[None, :]
    spread = jnp.broadcast_to(lengths[:, None], (own_rows, 128))
    f32, bf16 = jnp.float32, jnp.bfloat16
    dma = pltpu.SemaphoreType.DMA
    in_vmem = pl.BlockSpec(memory_space=pltpu.VMEM)
    anywhere = pl.BlockSpec(memory_space=pl.ANY)
    return pl.pallas_call(
        block_kernel,
        out_shape=jax.ShapeDtypeStruct((part_rows, out_cols), bf16),
        in_specs=[in_vmem] * 4 + [anywhere] * 4,
        out_specs=in_vmem,
        scratch_shapes=[
            pltpu.VMEM((8, part_rows, feats), bf16),
            pltpu.VMEM((RING, feats, col_width), bf16),
            pltpu.VMEM((part_rows + 16, col_width), f32),
            pltpu.VMEM((part_rows, 128), f32),
            pltpu.VMEM((part_rows, 128), f32),
            pltpu.VMEM((16, own_rows, col_width), f32),
            pltpu.VMEM((16, own_rows, col_width), f32),
            pltpu.VMEM((own_rows, full_cols), f32),
            pltpu.VMEM((own_rows, head_count, head_size), f32),
            pltpu.VMEM((own_rows, head_count, head_size), f32),
            pltpu.VMEM((8, 16, head_width // 4), f32),
            pltpu.VMEM((8, 16, head_width // 4), bf16),
            pltpu.VMEM((16, 16, head_width // 4), bf16),
            pltpu.VMEM((part_rows, head_width), f32),
            pltpu.VMEM((part_rows, head_width), bf16),
            pltpu.VMEM(key_cache.shape, bf16),
            pltpu.VMEM(value_cache.shape, bf16),
            pltpu.VMEM((8, head_width, out_cols), bf16),
            pltpu.VMEM((8, part_rows, out_cols), f32),
            pltpu.VMEM((4, part_rows, out_cols), f32),
            pltpu.VMEM((3, part_rows, out_cols), f32),
            dma((RING,)), dma((2,)), dma((8,)), dma((8,)), dma((8,)), dma, dma,
            dma((16,)), dma((16,)), dma((16,)), dma((16,)),
            dma((4,)), dma((4,)), dma((3,)), dma((3,)),
        ],
        compiler_params=pltpu.CompilerParams(
            collective_id=0, has_side_effects=True, vmem_limit_bytes=63 * 2**20
        ),
        cost_estimate=pl.CostEstimate(
            flops=2 * part_rows * (w_rows * col_width + head_width * out_width),
            bytes_accessed=2 * (w_rows * col_width + head_width * out_width),
            transcendentals=0,
        ),
        name="attention_block",
    )(
        hidden_in, jnp.cos(angle_now), jnp.sin(angle_now), spread,
        w_qkv, w_out, key_cache, value_cache,
    )


def solution(mesh):
    placed = (
        P("groups", "mp"),
        P("mp", None, None),
        P("mp", None, None),
        P(("groups", "mp"), None, None),
        P(("groups", "mp"), None, None),
        P(("groups", "mp")),
    )
    return jax.shard_map(
        shards, mesh=mesh, in_specs=placed, out_specs=P("groups", "mp"), check_vma=False
    )
```

```python
import jax
import jax.numpy as jnp
import numpy as np
from jax import lax
from jax.experimental import pallas as pl
from jax.experimental.pallas import tpu as pltpu
from jax.sharding import PartitionSpec as P

MESH = pl.DeviceIdType.MESH
D = 18432
COL_BITS = 3


def swapped(value, axis, bit):
    mask = 2**bit
    pairs = [(source, source ^ mask) for source in range(lax.axis_size(axis))]
    return lax.ppermute(value, axis, pairs)


def rotate(vectors, angle_now):
    half_dim = vectors.shape[-1] // 2
    front_half = vectors[..., :half_dim]
    back_half = vectors[..., half_dim:]
    cosine = jnp.cos(angle_now)
    sine_part = jnp.sin(angle_now)
    return jnp.concatenate(
        [front_half * cosine - back_half * sine_part, back_half * cosine + front_half * sine_part],
        -1,
    )


def cache_scores(query_part, key_cache, lengths):
    row_count = query_part.shape[0]
    head_size = key_cache.shape[-1]
    head_count = query_part.shape[1] // head_size
    half_dim = head_size // 2
    frequency = 10000.0 ** (-jnp.arange(half_dim, dtype=jnp.float32) / half_dim)
    angle_now = lengths.astype(jnp.float32)[:, None] * frequency[None, :]
    queries = rotate(
        query_part.reshape(row_count, head_count, head_size), angle_now[:, None, :]
    ).astype(jnp.bfloat16)
    score_scale = 1.0 / jnp.sqrt(jnp.float32(head_size))
    scores = (
        jnp.einsum("bhd,btd->bht", queries, key_cache, preferred_element_type=jnp.float32)
        * score_scale
    )
    live_mask = jnp.arange(key_cache.shape[1])[None, None, :] < lengths[:, None, None]
    return (queries, angle_now, jnp.where(live_mask, scores, -1e30))


def finish(queries, angle_now, scores, keyval_part, value_cache):
    row_count, head_count, head_size = queries.shape
    new_key = rotate(keyval_part[:, :head_size], angle_now).astype(jnp.bfloat16)
    new_value = keyval_part[:, head_size:].astype(jnp.bfloat16)
    score_scale = 1.0 / jnp.sqrt(jnp.float32(head_size))
    own_score = (
        jnp.sum(queries.astype(jnp.float32) * new_key.astype(jnp.float32)[:, None, :], -1)
        * score_scale
    )
    largest = jnp.maximum(jnp.max(scores, -1), own_score)
    weights = jnp.exp(scores - largest[..., None])
    own_weight = jnp.exp(own_score - largest)
    denominator = jnp.sum(weights, -1) + own_weight
    blended = jnp.einsum(
        "bht,btd->bhd",
        weights.astype(jnp.bfloat16),
        value_cache,
        preferred_element_type=jnp.float32,
    )
    blended = (
        blended
        + own_weight.astype(jnp.bfloat16).astype(jnp.float32)[..., None]
        * new_value.astype(jnp.float32)[:, None, :]
    )
    return (
        (blended / denominator[..., None])
        .reshape(row_count, head_count * head_size)
        .astype(jnp.bfloat16)
    )


def gather_features(block):
    device_index = lax.axis_index("mp")
    gathered = block
    for bit_level in range(COL_BITS):
        incoming = swapped(gathered, "mp", bit_level)
        mine_bit = device_index >> bit_level & 1
        gathered = jnp.where(
            mine_bit == 1,
            jnp.concatenate([incoming, gathered], 1),
            jnp.concatenate([gathered, incoming], 1),
        )
    return gathered


def reduce_rows(partial_value, high_bits):
    device_index = lax.axis_index("mp")
    total = partial_value
    for bit_level in reversed(range(COL_BITS, COL_BITS + high_bits)):
        half_rows = total.shape[0] // 2
        keep_back = device_index >> bit_level & 1 == 1
        outgoing = jnp.where(keep_back, total[:half_rows], total[half_rows:])
        staying = jnp.where(keep_back, total[half_rows:], total[:half_rows])
        total = staying + swapped(outgoing, "mp", bit_level)
    return total


def slots_to_holders(slots):
    device_index = lax.axis_index("mp")
    slot_count, row_count, width = slots.shape
    for bit_level in range(COL_BITS):
        shaped = slots.reshape(slot_count >> bit_level + 1, 2, 1 << bit_level, row_count, width)
        mine_bit = device_index >> bit_level & 1
        front_slots = shaped[:, 0]
        back_slots = shaped[:, 1]
        outgoing = jnp.where(mine_bit == 1, front_slots, back_slots)
        incoming = swapped(outgoing, "mp", bit_level)
        new_front = jnp.where(mine_bit == 1, incoming, front_slots)
        new_back = jnp.where(mine_bit == 1, back_slots, incoming)
        slots = jnp.stack([new_front, new_back], 1).reshape(slot_count, row_count, width)
    return slots


def reduce_features(partial_value):
    device_index = lax.axis_index("mp")
    total = partial_value
    for bit_level in reversed(range(COL_BITS)):
        half_cols = total.shape[1] // 2
        keep_back = device_index >> bit_level & 1 == 1
        outgoing = jnp.where(keep_back, total[:, :half_cols], total[:, half_cols:])
        staying = jnp.where(keep_back, total[:, half_cols:], total[:, :half_cols])
        total = staying + swapped(outgoing, "mp", bit_level)
    return total


def shards_plain(hidden_in, w_qkv, w_out, key_cache, value_cache, lengths):
    qkv_tile = w_qkv[0]
    out_tile = w_out[0]
    own_rows = key_cache.shape[0]
    head_size = key_cache.shape[2]
    tile_count = 1 << COL_BITS
    col_width = qkv_tile.shape[1]
    full_cols = col_width * tile_count
    width_q = full_cols - 2 * head_size
    head_width = out_tile.shape[0]
    high_bits = lax.axis_size("mp").bit_length() - 1 - COL_BITS
    device_index = lax.axis_index("mp")
    column_block = device_index & tile_count - 1
    wide_in = hidden_in.astype(jnp.float32)
    sums_local = jnp.sum(wide_in, 1)
    squares_local = jnp.sum(wide_in * wide_in, 1)
    ones_row = jnp.ones((1, qkv_tile.shape[0]), jnp.bfloat16)
    tile_columns = jnp.dot(ones_row, qkv_tile, preferred_element_type=jnp.float32)[0]
    columns_local = lax.dynamic_update_slice_in_dim(
        jnp.zeros((full_cols,), jnp.float32), tile_columns, column_block * col_width, 0
    )
    sums_all, squares_all, column_total = lax.psum((sums_local, squares_local, columns_local), "mp")
    first_row = device_index * own_rows
    row_sums = lax.dynamic_slice_in_dim(sums_all, first_row, own_rows)
    row_squares = lax.dynamic_slice_in_dim(squares_all, first_row, own_rows)
    row_mean = row_sums / D
    variance = row_squares / D - row_mean * row_mean
    inverse = lax.rsqrt(variance + 1e-05)
    feature_block = gather_features(hidden_in)
    partial_value = jnp.dot(feature_block, qkv_tile, preferred_element_type=jnp.float32)
    group_rows = reduce_rows(partial_value, high_bits)
    slots = group_rows.reshape(tile_count, own_rows, col_width)
    arrived = slots_to_holders(slots)
    raw_sums = jnp.transpose(arrived, (1, 0, 2)).reshape(own_rows, full_cols)
    projected = inverse[:, None] * (raw_sums - row_mean[:, None] * column_total[None, :])
    queries, angle_now, scores = cache_scores(projected[:, :width_q], key_cache, lengths)
    attended = finish(queries, angle_now, scores, projected[:, width_q:], value_cache)
    block_cols = lax.dynamic_slice_in_dim(
        lax.all_gather(attended, "mp", axis=0, tiled=True), column_block * head_width, head_width, 1
    )
    partial_out = jnp.dot(block_cols, out_tile, preferred_element_type=jnp.float32)
    outputs = reduce_features(partial_out)
    return outputs.astype(jnp.bfloat16)


RING = 8


def flipped(index, flips, bits):
    total = 0
    for level in range(bits):
        own_bit = index // 2**level % 2
        flip_bit = flips // 2**level % 2
        total = total + (own_bit + flip_bit - 2 * own_bit * flip_bit) * 2**level
    return total


def block_kernel(
    hid_ref, freq_ref, len_ref, wq_hbm, wo_hbm, key_hbm, val_hbm, out_ref,
    xb, wb, acc0, acc1, stat_send, stat_recv, psb0, psb1, prb0, prb1, pj, qf, attf, msgf, dsb, drb, lhsf, lhs,
    keys, vals, wo, pbuf, erecv, isend, irecv,
    w_sem, kv_sem, wo_sem, xs_sem, xr_sem, ss_sem, sr_sem, ps_sem, pr_sem,
    ds_sem, dr_sem, es_sem, er_sem, is_sem, ir_sem,
):
    me = lax.axis_index("mp")
    low = me % 8
    high = me // 8 * 8
    part_rows, feats = hid_ref.shape
    own_rows = len_ref.shape[0]
    halves = ((acc0, psb0, prb0), (acc1, psb1, prb1))
    starts = (0, acc0.shape[1])
    col_width = acc0.shape[1] + acc1.shape[1]
    head_size = qf.shape[2]
    head_count = qf.shape[1]
    half_dim = head_size // 2
    width_q = head_count * head_size
    out_cols = wo.shape[2]
    n_dev = 16

    def w_copy(half, step):
        cols = pl.ds(pl.multiple_of(flipped(low, step, 3) * feats, feats), feats)
        count = halves[half][0].shape[1]
        return pltpu.make_async_copy(
            wq_hbm.at[0, pl.ds(starts[half], count), cols],
            wb.at[step, pl.ds(0, count)],
            w_sem.at[half, step],
        )

    def wo_copy(block):
        cols = pl.ds(block * out_cols, out_cols)
        return pltpu.make_async_copy(wo_hbm.at[0, :, cols], wo.at[block], wo_sem.at[block])

    key_copy = pltpu.make_async_copy(key_hbm, keys, kv_sem.at[0])
    val_copy = pltpu.make_async_copy(val_hbm, vals, kv_sem.at[1])

    for step in range(RING):
        w_copy(0, step).start()

    barrier = pltpu.get_barrier_semaphore()
    for flips in range(1, n_dev):
        pl.semaphore_signal(
            barrier, inc=1, device_id={"mp": flipped(me, flips, 4)}, device_id_type=MESH
        )
    angle_now = len_ref[...].astype(jnp.float32) * freq_ref[...]
    cosines, sines = jnp.cos(angle_now), jnp.sin(angle_now)
    pl.semaphore_wait(barrier, n_dev - 1)

    def x_copy(source, flips, slot):
        return pltpu.make_async_remote_copy(
            src_ref=source, dst_ref=xb.at[slot], send_sem=xs_sem.at[slot],
            recv_sem=xr_sem.at[slot], device_id={"mp": high + flipped(low, flips, 3)},
            device_id_type=MESH,
        )

    for flips in (2, 4, 6, 1):
        x_copy(hid_ref, flips, flips).start()
    xb[0] = hid_ref[...]
    acc0[...] = jnp.zeros_like(acc0)
    acc1[...] = jnp.zeros_like(acc1)

    stat_copy = pltpu.make_async_remote_copy(
        src_ref=stat_send, dst_ref=stat_recv, send_sem=ss_sem, recv_sem=sr_sem,
        device_id={"mp": flipped(me, 8, 4)}, device_id_type=MESH,
    )

    def multiply(half, step):
        total = halves[half][0]
        w_copy(half, step).wait()
        with_ones = jnp.concatenate([xb[step], jnp.ones((16, feats), jnp.bfloat16)], 0)
        total[...] += lax.dot_general(
            with_ones,
            wb[step, : total.shape[1]],
            (((1,), (1,)), ((), ())),
            preferred_element_type=jnp.float32,
        )

    def first_body(step, sums):
        total, squares = sums

        @pl.when(step > 0)
        def _():
            x_copy(xb.at[step], 1, step).wait_recv()

        @pl.when((step >= 2) & (step % 2 == 0))
        def _():
            x_copy(xb.at[step], 1, step + 1).start()

        wide = xb[step].astype(jnp.float32)
        total = total + jnp.sum(wide, 1, keepdims=True)
        squares = squares + jnp.sum(wide * wide, 1, keepdims=True)

        @pl.when(step == 7)
        def _():
            lane = lax.broadcasted_iota(jnp.int32, stat_send.shape, 1)
            stat_send[...] = jnp.where(lane < 64, total, squares)
            stat_copy.start()

        multiply(0, step)
        w_copy(1, step).start()
        return (total, squares)

    def p_copy(half, flips):
        target = flipped(me, flips, 4)
        return pltpu.make_async_remote_copy(
            src_ref=halves[half][1].at[target], dst_ref=halves[half][2].at[me],
            send_sem=ps_sem.at[half, flips], recv_sem=pr_sem.at[half, flips],
            device_id={"mp": target}, device_id_type=MESH,
        )

    def p_arrival(half, flips):
        source = flipped(me, flips, 4)
        return pltpu.make_async_remote_copy(
            src_ref=halves[half][1].at[source], dst_ref=halves[half][2].at[source],
            send_sem=ps_sem.at[half, flips], recv_sem=pr_sem.at[half, flips],
            device_id={"mp": source}, device_id_type=MESH,
        )

    def send_half(half):
        total, outgoing, arriving = halves[half]
        both = stat_send[...] + stat_recv[...]
        row_mean = both[:, :1] / D
        variance = both[:, 64:65] / D - row_mean * row_mean
        inverse = lax.rsqrt(variance + 1e-05)
        projected = inverse * (total[:part_rows] - row_mean * total[part_rows : part_rows + 1])
        for dev in range(n_dev):
            outgoing[dev] = projected[dev * own_rows : (dev + 1) * own_rows]
        for flips in range(n_dev - 1, 0, -1):
            p_copy(half, flips).start()
        arriving[me] = outgoing[me]

    def second_body(step, carry):
        multiply(1, step)

        @pl.when(step == 0)
        def _():
            key_copy.start()
            val_copy.start()
            for block in range(4):
                wo_copy(block).start()
            stat_copy.wait()
            send_half(0)

        @pl.when(step == 3)
        def _():
            for block in range(4, 8):
                wo_copy(block).start()

        return carry

    nothing = jnp.zeros((part_rows, 1), jnp.float32)
    lax.fori_loop(0, 8, first_body, (nothing, nothing))
    lax.fori_loop(0, 8, second_body, 0)
    send_half(1)
    for half in range(2):
        arriving = halves[half][2]
        count = arriving.shape[2]
        for flips in range(1, n_dev):
            p_arrival(half, flips).wait_recv()
        for block in range(8):
            first = block * col_width + starts[half]
            pj[:, first : first + count] = arriving[block] + arriving[block + 8]
    for head in range(head_count):
        for row in range(own_rows):
            qf[row, head : head + 1, :] = pj[
                row : row + 1, head * head_size : (head + 1) * head_size
            ]

    key_copy.wait()
    val_copy.wait()
    scale = 1.0 / 16.0 if head_size == 256 else head_size**-0.5

    def turned(vectors, cosine, sine):
        front, back = vectors[:, :half_dim], vectors[:, half_dim:]
        return jnp.concatenate([front * cosine - back * sine, back * cosine + front * sine], 1)

    for row in range(own_rows):
        cosine, sine = cosines[row : row + 1], sines[row : row + 1]
        queries = turned(qf[row], cosine, sine).astype(jnp.bfloat16)
        new_key = turned(pj[row : row + 1, width_q : width_q + head_size], cosine, sine)
        new_key = new_key.astype(jnp.bfloat16).astype(jnp.float32)
        new_value = pj[row : row + 1, width_q + head_size :]
        new_value = new_value.astype(jnp.bfloat16).astype(jnp.float32)
        scores = scale * lax.dot_general(
            queries, keys[row], (((1,), (1,)), ((), ())), preferred_element_type=jnp.float32
        )
        slots = lax.broadcasted_iota(jnp.int32, scores.shape, 1)
        scores = jnp.where(slots < len_ref[row : row + 1, :1], scores, -1e30)
        own_score = scale * jnp.sum(queries.astype(jnp.float32) * new_key, 1, keepdims=True)
        largest = jnp.maximum(jnp.max(scores, 1, keepdims=True), own_score)
        weights = jnp.exp(scores - largest)
        own_weight = jnp.exp(own_score - largest)
        denominator = jnp.sum(weights, 1, keepdims=True) + own_weight
        blended = jnp.dot(
            weights.astype(jnp.bfloat16), vals[row], preferred_element_type=jnp.float32
        )
        blended = blended + own_weight.astype(jnp.bfloat16).astype(jnp.float32) * new_value
        attf[row] = blended / denominator

    parts = msgf.shape[1] // own_rows
    tiles = msgf.shape[2] // 128
    for block in range(8):
        for part in range(parts):
            for tile in range(tiles):
                column = ((block * parts + part) * tiles + tile) * 128
                head, lane = column // head_size, column % head_size
                for row in range(own_rows):
                    at = part * own_rows + row
                    msgf[block, at : at + 1, tile * 128 : (tile + 1) * 128] = attf[
                        row, head : head + 1, lane : lane + 128
                    ]
        dsb[block] = msgf[block].astype(jnp.bfloat16)

    def d_copy(flips):
        target = flipped(me, flips, 4)
        return pltpu.make_async_remote_copy(
            src_ref=dsb.at[target % 8], dst_ref=drb.at[me], send_sem=ds_sem.at[flips],
            recv_sem=dr_sem.at[flips], device_id={"mp": target}, device_id_type=MESH,
        )

    def d_arrival(flips):
        source = flipped(me, flips, 4)
        return pltpu.make_async_remote_copy(
            src_ref=dsb.at[source % 8], dst_ref=drb.at[source], send_sem=ds_sem.at[flips],
            recv_sem=dr_sem.at[flips], device_id={"mp": source}, device_id_type=MESH,
        )

    for flips in range(n_dev - 1, 0, -1):
        d_copy(flips).start()
    drb[me] = dsb[low]
    for flips in range(1, n_dev):
        d_arrival(flips).wait_recv()
    width = msgf.shape[2]
    for dev in range(n_dev):
        arrived = drb[dev].astype(jnp.float32)
        for part in range(parts):
            lhsf[dev * own_rows : (dev + 1) * own_rows, part * width : (part + 1) * width] = (
                arrived[part * own_rows : (part + 1) * own_rows]
            )
    lhs[...] = lhsf[...].astype(jnp.bfloat16)
    for block in range(8):
        wo_copy(block).wait()

    def e_copy(turn):
        return pltpu.make_async_remote_copy(
            src_ref=pbuf.at[2 * turn], dst_ref=erecv.at[turn], send_sem=es_sem.at[turn],
            recv_sem=er_sem.at[turn], device_id={"mp": flipped(me, 1, 4)}, device_id_type=MESH,
        )

    def i_copy(turn):
        return pltpu.make_async_remote_copy(
            src_ref=isend.at[turn], dst_ref=irecv.at[turn], send_sem=is_sem.at[turn],
            recv_sem=ir_sem.at[turn],
            device_id={"mp": high + flipped(low, 6 - 2 * turn, 3)}, device_id_type=MESH,
        )

    def out_body(turn, carry):
        flips = 6 - 2 * turn
        pbuf[2 * turn] = jnp.dot(
            lhs[...], wo[flipped(low, flips + 1, 3)], preferred_element_type=jnp.float32
        )
        e_copy(turn).start()
        pbuf[2 * turn + 1] = jnp.dot(
            lhs[...], wo[flipped(low, flips, 3)], preferred_element_type=jnp.float32
        )
        e_copy(turn).wait_recv()
        pbuf[2 * turn + 1] += erecv[turn]

        @pl.when(turn < 3)
        def _():
            isend[turn] = pbuf[2 * turn + 1].astype(jnp.bfloat16)
            i_copy(turn).start()

        return carry

    lax.fori_loop(0, 4, out_body, 0)
    for turn in range(3):
        i_copy(turn).wait_recv()
    total = pbuf[7]
    for turn in range(3):
        total = total + irecv[turn].astype(jnp.float32)
    out_ref[...] = total.astype(jnp.bfloat16)

    for slot in range(1, 8):
        x_copy(hid_ref, 1, slot).wait_send()
    for flips in range(1, n_dev):
        p_copy(0, flips).wait_send()
        p_copy(1, flips).wait_send()
        d_copy(flips).wait_send()
    for turn in range(4):
        e_copy(turn).wait_send()
    for turn in range(3):
        i_copy(turn).wait_send()


def shards(hidden_in, w_qkv, w_out, key_cache, value_cache, lengths):
    part_rows, feats = hidden_in.shape
    own_rows, slot_count, head_size = key_cache.shape
    _, w_rows, col_width = w_qkv.shape
    _, head_width, out_width = w_out.shape
    if (
        lax.axis_size("mp") != 16
        or w_rows != 8 * feats
        or own_rows != 4
        or part_rows != 64
        or feats % 128 != 0
        or head_width % 512 != 0
        or head_size != 256
        or col_width % 64 != 0
    ):
        return shards_plain(hidden_in, w_qkv, w_out, key_cache, value_cache, lengths)
    half_dim = head_size // 2
    out_cols = out_width // 8
    full_cols = col_width * 8
    head_count = head_width * 8 // head_size
    frequency = np.power(10000.0, -np.arange(half_dim) / half_dim).astype(np.float32)[None]
    width0 = col_width // 512 * 256
    width1 = col_width - width0
    spread = jnp.broadcast_to(lengths[:, None], (own_rows, 128))
    f32, bf16 = jnp.float32, jnp.bfloat16
    dma = pltpu.SemaphoreType.DMA
    in_vmem = pl.BlockSpec(memory_space=pltpu.VMEM)
    anywhere = pl.BlockSpec(memory_space=pl.ANY)
    return pl.pallas_call(
        block_kernel,
        out_shape=jax.ShapeDtypeStruct((part_rows, out_cols), bf16),
        in_specs=[in_vmem] * 3 + [anywhere] * 4,
        out_specs=in_vmem,
        scratch_shapes=[
            pltpu.VMEM((8, part_rows, feats), bf16),
            pltpu.VMEM((RING, width1, feats), bf16),
            pltpu.VMEM((part_rows + 16, width0), f32),
            pltpu.VMEM((part_rows + 16, width1), f32),
            pltpu.VMEM((part_rows, 128), f32),
            pltpu.VMEM((part_rows, 128), f32),
            pltpu.VMEM((16, own_rows, width0), f32),
            pltpu.VMEM((16, own_rows, width1), f32),
            pltpu.VMEM((16, own_rows, width0), f32),
            pltpu.VMEM((16, own_rows, width1), f32),
            pltpu.VMEM((own_rows, full_cols), f32),
            pltpu.VMEM((own_rows, head_count, head_size), f32),
            pltpu.VMEM((own_rows, head_count, head_size), f32),
            pltpu.VMEM((8, 16, head_width // 4), f32),
            pltpu.VMEM((8, 16, head_width // 4), bf16),
            pltpu.VMEM((16, 16, head_width // 4), bf16),
            pltpu.VMEM((part_rows, head_width), f32),
            pltpu.VMEM((part_rows, head_width), bf16),
            pltpu.VMEM(key_cache.shape, bf16),
            pltpu.VMEM(value_cache.shape, bf16),
            pltpu.VMEM((8, head_width, out_cols), bf16),
            pltpu.VMEM((8, part_rows, out_cols), f32),
            pltpu.VMEM((4, part_rows, out_cols), f32),
            pltpu.VMEM((3, part_rows, out_cols), bf16),
            pltpu.VMEM((3, part_rows, out_cols), bf16),
            dma((2, RING)), dma((2,)), dma((8,)), dma((8,)), dma((8,)), dma, dma,
            dma((2, 16)), dma((2, 16)), dma((16,)), dma((16,)),
            dma((4,)), dma((4,)), dma((3,)), dma((3,)),
        ],
        compiler_params=pltpu.CompilerParams(
            collective_id=0, has_side_effects=True, vmem_limit_bytes=63 * 2**20
        ),
        cost_estimate=pl.CostEstimate(
            flops=2 * part_rows * (w_rows * col_width + head_width * out_width),
            bytes_accessed=2 * (w_rows * col_width + head_width * out_width),
            transcendentals=0,
        ),
        name="attention_block",
    )(
        hidden_in, jnp.asarray(frequency), spread,
        jnp.swapaxes(w_qkv, 1, 2), w_out, key_cache, value_cache,
    )


def solution(mesh):
    placed = (
        P("groups", "mp"),
        P("mp", None, None),
        P("mp", None, None),
        P(("groups", "mp"), None, None),
        P(("groups", "mp"), None, None),
        P(("groups", "mp")),
    )
    return jax.shard_map(
        shards, mesh=mesh, in_specs=placed, out_specs=P("groups", "mp"), check_vma=False
    )
```

```python
import jax
import jax.numpy as jnp
import numpy as np
from jax import lax
from jax.experimental import pallas as pl
from jax.experimental.pallas import tpu as pltpu
from jax.sharding import PartitionSpec as P

MESH = pl.DeviceIdType.MESH
D = 18432
COL_BITS = 3


def swapped(value, axis, bit):
    mask = 2**bit
    pairs = [(source, source ^ mask) for source in range(lax.axis_size(axis))]
    return lax.ppermute(value, axis, pairs)


def rotate(vectors, angle_now):
    half_dim = vectors.shape[-1] // 2
    front_half = vectors[..., :half_dim]
    back_half = vectors[..., half_dim:]
    cosine = jnp.cos(angle_now)
    sine_part = jnp.sin(angle_now)
    return jnp.concatenate(
        [front_half * cosine - back_half * sine_part, back_half * cosine + front_half * sine_part],
        -1,
    )


def cache_scores(query_part, key_cache, lengths):
    row_count = query_part.shape[0]
    head_size = key_cache.shape[-1]
    head_count = query_part.shape[1] // head_size
    half_dim = head_size // 2
    frequency = 10000.0 ** (-jnp.arange(half_dim, dtype=jnp.float32) / half_dim)
    angle_now = lengths.astype(jnp.float32)[:, None] * frequency[None, :]
    queries = rotate(
        query_part.reshape(row_count, head_count, head_size), angle_now[:, None, :]
    ).astype(jnp.bfloat16)
    score_scale = 1.0 / jnp.sqrt(jnp.float32(head_size))
    scores = (
        jnp.einsum("bhd,btd->bht", queries, key_cache, preferred_element_type=jnp.float32)
        * score_scale
    )
    live_mask = jnp.arange(key_cache.shape[1])[None, None, :] < lengths[:, None, None]
    return (queries, angle_now, jnp.where(live_mask, scores, -1e30))


def finish(queries, angle_now, scores, keyval_part, value_cache):
    row_count, head_count, head_size = queries.shape
    new_key = rotate(keyval_part[:, :head_size], angle_now).astype(jnp.bfloat16)
    new_value = keyval_part[:, head_size:].astype(jnp.bfloat16)
    score_scale = 1.0 / jnp.sqrt(jnp.float32(head_size))
    own_score = (
        jnp.sum(queries.astype(jnp.float32) * new_key.astype(jnp.float32)[:, None, :], -1)
        * score_scale
    )
    largest = jnp.maximum(jnp.max(scores, -1), own_score)
    weights = jnp.exp(scores - largest[..., None])
    own_weight = jnp.exp(own_score - largest)
    denominator = jnp.sum(weights, -1) + own_weight
    blended = jnp.einsum(
        "bht,btd->bhd",
        weights.astype(jnp.bfloat16),
        value_cache,
        preferred_element_type=jnp.float32,
    )
    blended = (
        blended
        + own_weight.astype(jnp.bfloat16).astype(jnp.float32)[..., None]
        * new_value.astype(jnp.float32)[:, None, :]
    )
    return (
        (blended / denominator[..., None])
        .reshape(row_count, head_count * head_size)
        .astype(jnp.bfloat16)
    )


def gather_features(block):
    device_index = lax.axis_index("mp")
    gathered = block
    for bit_level in range(COL_BITS):
        incoming = swapped(gathered, "mp", bit_level)
        mine_bit = device_index >> bit_level & 1
        gathered = jnp.where(
            mine_bit == 1,
            jnp.concatenate([incoming, gathered], 1),
            jnp.concatenate([gathered, incoming], 1),
        )
    return gathered


def reduce_rows(partial_value, high_bits):
    device_index = lax.axis_index("mp")
    total = partial_value
    for bit_level in reversed(range(COL_BITS, COL_BITS + high_bits)):
        half_rows = total.shape[0] // 2
        keep_back = device_index >> bit_level & 1 == 1
        outgoing = jnp.where(keep_back, total[:half_rows], total[half_rows:])
        staying = jnp.where(keep_back, total[half_rows:], total[:half_rows])
        total = staying + swapped(outgoing, "mp", bit_level)
    return total


def slots_to_holders(slots):
    device_index = lax.axis_index("mp")
    slot_count, row_count, width = slots.shape
    for bit_level in range(COL_BITS):
        shaped = slots.reshape(slot_count >> bit_level + 1, 2, 1 << bit_level, row_count, width)
        mine_bit = device_index >> bit_level & 1
        front_slots = shaped[:, 0]
        back_slots = shaped[:, 1]
        outgoing = jnp.where(mine_bit == 1, front_slots, back_slots)
        incoming = swapped(outgoing, "mp", bit_level)
        new_front = jnp.where(mine_bit == 1, incoming, front_slots)
        new_back = jnp.where(mine_bit == 1, back_slots, incoming)
        slots = jnp.stack([new_front, new_back], 1).reshape(slot_count, row_count, width)
    return slots


def reduce_features(partial_value):
    device_index = lax.axis_index("mp")
    total = partial_value
    for bit_level in reversed(range(COL_BITS)):
        half_cols = total.shape[1] // 2
        keep_back = device_index >> bit_level & 1 == 1
        outgoing = jnp.where(keep_back, total[:, :half_cols], total[:, half_cols:])
        staying = jnp.where(keep_back, total[:, half_cols:], total[:, :half_cols])
        total = staying + swapped(outgoing, "mp", bit_level)
    return total


def shards_plain(hidden_in, w_qkv, w_out, key_cache, value_cache, lengths):
    qkv_tile = w_qkv[0]
    out_tile = w_out[0]
    own_rows = key_cache.shape[0]
    head_size = key_cache.shape[2]
    tile_count = 1 << COL_BITS
    col_width = qkv_tile.shape[1]
    full_cols = col_width * tile_count
    width_q = full_cols - 2 * head_size
    head_width = out_tile.shape[0]
    high_bits = lax.axis_size("mp").bit_length() - 1 - COL_BITS
    device_index = lax.axis_index("mp")
    column_block = device_index & tile_count - 1
    wide_in = hidden_in.astype(jnp.float32)
    sums_local = jnp.sum(wide_in, 1)
    squares_local = jnp.sum(wide_in * wide_in, 1)
    ones_row = jnp.ones((1, qkv_tile.shape[0]), jnp.bfloat16)
    tile_columns = jnp.dot(ones_row, qkv_tile, preferred_element_type=jnp.float32)[0]
    columns_local = lax.dynamic_update_slice_in_dim(
        jnp.zeros((full_cols,), jnp.float32), tile_columns, column_block * col_width, 0
    )
    sums_all, squares_all, column_total = lax.psum((sums_local, squares_local, columns_local), "mp")
    first_row = device_index * own_rows
    row_sums = lax.dynamic_slice_in_dim(sums_all, first_row, own_rows)
    row_squares = lax.dynamic_slice_in_dim(squares_all, first_row, own_rows)
    row_mean = row_sums / D
    variance = row_squares / D - row_mean * row_mean
    inverse = lax.rsqrt(variance + 1e-05)
    feature_block = gather_features(hidden_in)
    partial_value = jnp.dot(feature_block, qkv_tile, preferred_element_type=jnp.float32)
    group_rows = reduce_rows(partial_value, high_bits)
    slots = group_rows.reshape(tile_count, own_rows, col_width)
    arrived = slots_to_holders(slots)
    raw_sums = jnp.transpose(arrived, (1, 0, 2)).reshape(own_rows, full_cols)
    projected = inverse[:, None] * (raw_sums - row_mean[:, None] * column_total[None, :])
    queries, angle_now, scores = cache_scores(projected[:, :width_q], key_cache, lengths)
    attended = finish(queries, angle_now, scores, projected[:, width_q:], value_cache)
    block_cols = lax.dynamic_slice_in_dim(
        lax.all_gather(attended, "mp", axis=0, tiled=True), column_block * head_width, head_width, 1
    )
    partial_out = jnp.dot(block_cols, out_tile, preferred_element_type=jnp.float32)
    outputs = reduce_features(partial_out)
    return outputs.astype(jnp.bfloat16)


RING = 8


def flipped(index, flips, bits):
    total = 0
    for level in range(bits):
        own_bit = index // 2**level % 2
        flip_bit = flips // 2**level % 2
        total = total + (own_bit + flip_bit - 2 * own_bit * flip_bit) * 2**level
    return total


def block_kernel(
    hid_ref, freq_ref, len_ref, wq_hbm, wo_hbm, key_hbm, val_hbm, out_ref,
    xb, wb, acc0, acc1, stat_send, stat_recv, psb0, psb1, prb0, prb1, pj, qf, attf, msgf, dsb, drb, lhsf, lhs,
    keys, vals, wo, pbuf, erecv, isend, irecv,
    w_sem, kv_sem, wo_sem, xs_sem, xr_sem, ss_sem, sr_sem, ps_sem, pr_sem,
    ds_sem, dr_sem, es_sem, er_sem, is_sem, ir_sem,
):
    me = lax.axis_index("mp")
    low = me % 8
    high = me // 8 * 8
    part_rows, feats = hid_ref.shape
    own_rows = len_ref.shape[0]
    halves = ((acc0, psb0, prb0), (acc1, psb1, prb1))
    starts = (0, acc0.shape[1])
    col_width = acc0.shape[1] + acc1.shape[1]
    head_size = qf.shape[2]
    head_count = qf.shape[1]
    half_dim = head_size // 2
    width_q = head_count * head_size
    out_cols = wo.shape[2]
    n_dev = 16

    def w_copy(half, step):
        cols = pl.ds(pl.multiple_of(flipped(low, step, 3) * feats, feats), feats)
        count = halves[half][0].shape[1]
        return pltpu.make_async_copy(
            wq_hbm.at[0, pl.ds(starts[half], count), cols],
            wb.at[step, pl.ds(0, count)],
            w_sem.at[half, step],
        )

    def wo_copy(block):
        cols = pl.ds(block * out_cols, out_cols)
        return pltpu.make_async_copy(wo_hbm.at[0, :, cols], wo.at[block], wo_sem.at[block])

    key_copy = pltpu.make_async_copy(key_hbm, keys, kv_sem.at[0])
    val_copy = pltpu.make_async_copy(val_hbm, vals, kv_sem.at[1])

    for step in range(RING):
        w_copy(0, step).start()
    key_copy.start()
    val_copy.start()

    barrier = pltpu.get_barrier_semaphore()
    for flips in range(1, n_dev):
        pl.semaphore_signal(
            barrier, inc=1, device_id={"mp": flipped(me, flips, 4)}, device_id_type=MESH
        )
    angle_now = jnp.concatenate(
        [len_ref[row].astype(jnp.float32) * freq_ref[...] for row in range(own_rows)], 0
    )
    cosines, sines = jnp.cos(angle_now), jnp.sin(angle_now)
    pl.semaphore_wait(barrier, n_dev - 1)

    def x_copy(source, flips, slot):
        return pltpu.make_async_remote_copy(
            src_ref=source, dst_ref=xb.at[slot], send_sem=xs_sem.at[slot],
            recv_sem=xr_sem.at[slot], device_id={"mp": high + flipped(low, flips, 3)},
            device_id_type=MESH,
        )

    for flips in (2, 4, 6, 1):
        x_copy(hid_ref, flips, flips).start()
    for block in range(8):
        wo_copy(block).start()
    xb[0] = hid_ref[...]
    acc0[...] = jnp.zeros_like(acc0)
    acc1[...] = jnp.zeros_like(acc1)

    stat_copy = pltpu.make_async_remote_copy(
        src_ref=stat_send, dst_ref=stat_recv, send_sem=ss_sem, recv_sem=sr_sem,
        device_id={"mp": flipped(me, 8, 4)}, device_id_type=MESH,
    )

    def multiply(half, step):
        total = halves[half][0]
        w_copy(half, step).wait()
        with_ones = jnp.concatenate([xb[step], jnp.ones((16, feats), jnp.bfloat16)], 0)
        total[...] += lax.dot_general(
            with_ones,
            wb[step, : total.shape[1]],
            (((1,), (1,)), ((), ())),
            preferred_element_type=jnp.float32,
        )

    def first_body(step, sums):
        total, squares = sums

        @pl.when(step > 0)
        def _():
            x_copy(xb.at[step], 1, step).wait_recv()

        @pl.when((step >= 2) & (step % 2 == 0))
        def _():
            x_copy(xb.at[step], 1, step + 1).start()

        wide = xb[step].astype(jnp.float32)
        total = total + jnp.sum(wide, 1, keepdims=True)
        squares = squares + jnp.sum(wide * wide, 1, keepdims=True)

        @pl.when(step == 7)
        def _():
            lane = lax.broadcasted_iota(jnp.int32, stat_send.shape, 1)
            stat_send[...] = jnp.where(lane < 64, total, squares)
            stat_copy.start()

        multiply(0, step)
        w_copy(1, step).start()
        return (total, squares)

    def p_copy(half, flips):
        target = flipped(me, flips, 4)
        return pltpu.make_async_remote_copy(
            src_ref=halves[half][1].at[target], dst_ref=halves[half][2].at[me],
            send_sem=ps_sem.at[half, flips], recv_sem=pr_sem.at[half, flips],
            device_id={"mp": target}, device_id_type=MESH,
        )

    def p_arrival(half, flips):
        source = flipped(me, flips, 4)
        return pltpu.make_async_remote_copy(
            src_ref=halves[half][1].at[source], dst_ref=halves[half][2].at[source],
            send_sem=ps_sem.at[half, flips], recv_sem=pr_sem.at[half, flips],
            device_id={"mp": source}, device_id_type=MESH,
        )

    def send_half(half):
        total, outgoing, arriving = halves[half]
        both = stat_send[...] + stat_recv[...]
        row_mean = both[:, :1] / D
        variance = both[:, 64:65] / D - row_mean * row_mean
        inverse = lax.rsqrt(variance + 1e-05)
        projected = inverse * (total[:part_rows] - row_mean * total[part_rows : part_rows + 1])
        for dev in range(n_dev):
            outgoing[dev] = projected[dev * own_rows : (dev + 1) * own_rows]
        for flips in range(n_dev - 1, 0, -1):
            p_copy(half, flips).start()
        arriving[me] = outgoing[me]

    def second_body(step, carry):
        multiply(1, step)

        @pl.when(step == 0)
        def _():
            stat_copy.wait()
            send_half(0)

        return carry

    nothing = jnp.zeros((part_rows, 1), jnp.float32)
    lax.fori_loop(0, 8, first_body, (nothing, nothing))
    lax.fori_loop(0, 8, second_body, 0)
    send_half(1)
    for half in range(2):
        arriving = halves[half][2]
        count = arriving.shape[2]
        for flips in range(1, n_dev):
            p_arrival(half, flips).wait_recv()
        for block in range(8):
            first = block * col_width + starts[half]
            pj[:, first : first + count] = arriving[block] + arriving[block + 8]
    for head in range(head_count):
        for row in range(own_rows):
            qf[row, head : head + 1, :] = pj[
                row : row + 1, head * head_size : (head + 1) * head_size
            ]

    key_copy.wait()
    val_copy.wait()
    scale = 1.0 / 16.0 if head_size == 256 else head_size**-0.5

    def turned(vectors, cosine, sine):
        front, back = vectors[:, :half_dim], vectors[:, half_dim:]
        return jnp.concatenate([front * cosine - back * sine, back * cosine + front * sine], 1)

    for row in range(own_rows):
        cosine, sine = cosines[row : row + 1], sines[row : row + 1]
        queries = turned(qf[row], cosine, sine).astype(jnp.bfloat16)
        new_key = turned(pj[row : row + 1, width_q : width_q + head_size], cosine, sine)
        new_key = new_key.astype(jnp.bfloat16).astype(jnp.float32)
        new_value = pj[row : row + 1, width_q + head_size :]
        new_value = new_value.astype(jnp.bfloat16).astype(jnp.float32)
        scores = scale * lax.dot_general(
            queries, keys[row], (((1,), (1,)), ((), ())), preferred_element_type=jnp.float32
        )
        slots = lax.broadcasted_iota(jnp.int32, scores.shape, 1)
        scores = jnp.where(slots < len_ref[row], scores, -1e30)
        own_score = scale * jnp.sum(queries.astype(jnp.float32) * new_key, 1, keepdims=True)
        largest = jnp.maximum(jnp.max(scores, 1, keepdims=True), own_score)
        weights = jnp.exp(scores - largest)
        own_weight = jnp.exp(own_score - largest)
        denominator = jnp.sum(weights, 1, keepdims=True) + own_weight
        blended = jnp.dot(
            weights.astype(jnp.bfloat16), vals[row], preferred_element_type=jnp.float32
        )
        blended = blended + own_weight.astype(jnp.bfloat16).astype(jnp.float32) * new_value
        attf[row] = blended / denominator

    parts = msgf.shape[1] // own_rows
    tiles = msgf.shape[2] // 128
    for block in range(8):
        for part in range(parts):
            for tile in range(tiles):
                column = ((block * parts + part) * tiles + tile) * 128
                head, lane = column // head_size, column % head_size
                for row in range(own_rows):
                    at = part * own_rows + row
                    msgf[block, at : at + 1, tile * 128 : (tile + 1) * 128] = attf[
                        row, head : head + 1, lane : lane + 128
                    ]
        dsb[block] = msgf[block].astype(jnp.bfloat16)

    def d_copy(flips):
        target = flipped(me, flips, 4)
        return pltpu.make_async_remote_copy(
            src_ref=dsb.at[target % 8], dst_ref=drb.at[me], send_sem=ds_sem.at[flips],
            recv_sem=dr_sem.at[flips], device_id={"mp": target}, device_id_type=MESH,
        )

    def d_arrival(flips):
        source = flipped(me, flips, 4)
        return pltpu.make_async_remote_copy(
            src_ref=dsb.at[source % 8], dst_ref=drb.at[source], send_sem=ds_sem.at[flips],
            recv_sem=dr_sem.at[flips], device_id={"mp": source}, device_id_type=MESH,
        )

    for flips in range(n_dev - 1, 0, -1):
        d_copy(flips).start()
    drb[me] = dsb[low]
    for flips in range(1, n_dev):
        d_arrival(flips).wait_recv()
    width = msgf.shape[2]
    for dev in range(n_dev):
        arrived = drb[dev].astype(jnp.float32)
        for part in range(parts):
            lhsf[dev * own_rows : (dev + 1) * own_rows, part * width : (part + 1) * width] = (
                arrived[part * own_rows : (part + 1) * own_rows]
            )
    lhs[...] = lhsf[...].astype(jnp.bfloat16)
    for block in range(8):
        wo_copy(block).wait()

    def e_copy(turn):
        return pltpu.make_async_remote_copy(
            src_ref=pbuf.at[2 * turn], dst_ref=erecv.at[turn], send_sem=es_sem.at[turn],
            recv_sem=er_sem.at[turn], device_id={"mp": flipped(me, 1, 4)}, device_id_type=MESH,
        )

    def i_copy(turn):
        return pltpu.make_async_remote_copy(
            src_ref=isend.at[turn], dst_ref=irecv.at[turn], send_sem=is_sem.at[turn],
            recv_sem=ir_sem.at[turn],
            device_id={"mp": high + flipped(low, 6 - 2 * turn, 3)}, device_id_type=MESH,
        )

    def out_body(turn, carry):
        flips = 6 - 2 * turn
        pbuf[2 * turn] = jnp.dot(
            lhs[...], wo[flipped(low, flips + 1, 3)], preferred_element_type=jnp.float32
        )
        e_copy(turn).start()
        pbuf[2 * turn + 1] = jnp.dot(
            lhs[...], wo[flipped(low, flips, 3)], preferred_element_type=jnp.float32
        )
        e_copy(turn).wait_recv()
        pbuf[2 * turn + 1] += erecv[turn]

        @pl.when(turn < 3)
        def _():
            isend[turn] = pbuf[2 * turn + 1].astype(jnp.bfloat16)
            i_copy(turn).start()

        return carry

    lax.fori_loop(0, 4, out_body, 0)
    for turn in range(3):
        i_copy(turn).wait_recv()
    total = pbuf[7]
    for turn in range(3):
        total = total + irecv[turn].astype(jnp.float32)
    out_ref[...] = total.astype(jnp.bfloat16)

    for slot in range(1, 8):
        x_copy(hid_ref, 1, slot).wait_send()
    for flips in range(1, n_dev):
        p_copy(0, flips).wait_send()
        p_copy(1, flips).wait_send()
        d_copy(flips).wait_send()
    for turn in range(4):
        e_copy(turn).wait_send()
    for turn in range(3):
        i_copy(turn).wait_send()


def shards(hidden_in, w_qkv, w_out, key_cache, value_cache, lengths):
    part_rows, feats = hidden_in.shape
    own_rows, slot_count, head_size = key_cache.shape
    _, w_rows, col_width = w_qkv.shape
    _, head_width, out_width = w_out.shape
    if (
        lax.axis_size("mp") != 16
        or w_rows != 8 * feats
        or own_rows != 4
        or part_rows != 64
        or feats % 128 != 0
        or head_width % 512 != 0
        or head_size != 256
        or col_width % 64 != 0
    ):
        return shards_plain(hidden_in, w_qkv, w_out, key_cache, value_cache, lengths)
    half_dim = head_size // 2
    out_cols = out_width // 8
    full_cols = col_width * 8
    head_count = head_width * 8 // head_size
    frequency = np.power(10000.0, -np.arange(half_dim) / half_dim).astype(np.float32)[None]
    width0 = col_width // 512 * 256
    width1 = col_width - width0
    f32, bf16 = jnp.float32, jnp.bfloat16
    dma = pltpu.SemaphoreType.DMA
    in_vmem = pl.BlockSpec(memory_space=pltpu.VMEM)
    anywhere = pl.BlockSpec(memory_space=pl.ANY)
    return pl.pallas_call(
        block_kernel,
        out_shape=jax.ShapeDtypeStruct((part_rows, out_cols), bf16),
        in_specs=[in_vmem, in_vmem, pl.BlockSpec(memory_space=pltpu.SMEM)] + [anywhere] * 4,
        out_specs=in_vmem,
        scratch_shapes=[
            pltpu.VMEM((8, part_rows, feats), bf16),
            pltpu.VMEM((RING, width1, feats), bf16),
            pltpu.VMEM((part_rows + 16, width0), f32),
            pltpu.VMEM((part_rows + 16, width1), f32),
            pltpu.VMEM((part_rows, 128), f32),
            pltpu.VMEM((part_rows, 128), f32),
            pltpu.VMEM((16, own_rows, width0), f32),
            pltpu.VMEM((16, own_rows, width1), f32),
            pltpu.VMEM((16, own_rows, width0), f32),
            pltpu.VMEM((16, own_rows, width1), f32),
            pltpu.VMEM((own_rows, full_cols), f32),
            pltpu.VMEM((own_rows, head_count, head_size), f32),
            pltpu.VMEM((own_rows, head_count, head_size), f32),
            pltpu.VMEM((8, 16, head_width // 4), f32),
            pltpu.VMEM((8, 16, head_width // 4), bf16),
            pltpu.VMEM((16, 16, head_width // 4), bf16),
            pltpu.VMEM((part_rows, head_width), f32),
            pltpu.VMEM((part_rows, head_width), bf16),
            pltpu.VMEM(key_cache.shape, bf16),
            pltpu.VMEM(value_cache.shape, bf16),
            pltpu.VMEM((8, head_width, out_cols), bf16),
            pltpu.VMEM((8, part_rows, out_cols), f32),
            pltpu.VMEM((4, part_rows, out_cols), f32),
            pltpu.VMEM((3, part_rows, out_cols), bf16),
            pltpu.VMEM((3, part_rows, out_cols), bf16),
            dma((2, RING)), dma((2,)), dma((8,)), dma((8,)), dma((8,)), dma, dma,
            dma((2, 16)), dma((2, 16)), dma((16,)), dma((16,)),
            dma((4,)), dma((4,)), dma((3,)), dma((3,)),
        ],
        compiler_params=pltpu.CompilerParams(
            collective_id=0, has_side_effects=True, vmem_limit_bytes=63 * 2**20
        ),
        cost_estimate=pl.CostEstimate(
            flops=2 * part_rows * (w_rows * col_width + head_width * out_width),
            bytes_accessed=2 * (w_rows * col_width + head_width * out_width),
            transcendentals=0,
        ),
        name="attention_block",
    )(
        hidden_in, jnp.asarray(frequency), lengths,
        jnp.swapaxes(w_qkv, 1, 2), w_out, key_cache, value_cache,
    )


def solution(mesh):
    placed = (
        P("groups", "mp"),
        P("mp", None, None),
        P("mp", None, None),
        P(("groups", "mp"), None, None),
        P(("groups", "mp"), None, None),
        P(("groups", "mp")),
    )
    return jax.shard_map(
        shards, mesh=mesh, in_specs=placed, out_specs=P("groups", "mp"), check_vma=False
    )
```
